32 devices in a mesh: task: 4 (over y, core), row: 8 (over z, x).
Axes of the slice: x: 2, y: 2, z: 4, core: 2. Of those that a mesh axis runs over, the one named last changes fastest.
Arguments:
- deltas: bfloat16 [8, 25600, 5120], P('task', 'row'), may hold values from -20 to 20, as said below
- sketch: bfloat16 [25600, 128], P('row'), may hold values from -0.0390625 to 0.0390625
Outputs:
- merged: bfloat16 [25600, 5120], P('row', 'task')
The draws below stay inside these ranges and needn't reach their ends.
Inputs may be any that keep to these rules, and one draw needn't show every extreme that they name: Real-valued deltas; the tasks share part of their structure.
All inputs are finite; a program needn't handle non-finite values.
Results may differ from the reference program's by a relative error of at most 0.04.
Values may be sent and summed in bfloat16 or wider, within the bound.
A program may use at most 192 MiB of HBM per device.

```python
import jax
import jax.numpy as jnp
from jax import lax

D = 5120
FF = 25600
RANK = 128
NS_STEPS = 5
TASKS = 8


def draw_deltas(key, part):
    key = jax.random.fold_in(key, 7)
    shared_key, own_key = jax.random.split(key)
    shared = jax.random.normal(shared_key, (FF, D), jnp.float32)
    own = jax.random.normal(own_key, (TASKS, FF, D), jnp.float32)
    blended = 0.8 * shared[None] + 0.6 * own
    levels = 3.0 ** (jnp.arange(TASKS, dtype=jnp.float32) / (TASKS - 1))
    return jnp.clip(blended * levels[:, None, None], -20.0, 20.0).astype(jnp.bfloat16)


def level_of(key, shape, cuts, least, high):
    factor_of = 1.0
    for axis_at, shards_of in cuts:
        steps = jax.random.uniform(jax.random.fold_in(jax.random.fold_in(key, 6), axis_at), (shards_of,), jnp.float32, least / len(cuts), high / len(cuts))
        factor_of = factor_of * jnp.repeat(jnp.exp(steps), shape[axis_at] // shards_of).reshape((-1,) + (1,) * (len(shape) - 1 - axis_at))
    return factor_of


def gaussian(stream_key, dims, spread, bound, pieces=(), kind=jnp.bfloat16):
    array = spread * jax.random.normal(stream_key, dims, jnp.float32)
    if pieces:
        array = array * level_of(stream_key, dims, pieces, -0.22, 0.18)
    return jnp.clip(array, -bound, bound).astype(kind)


def setup_inputs(seed: int = 0) -> dict:
    streams_of = jax.random.split(jax.random.key(seed), 3)
    deltas = draw_deltas(jax.random.fold_in(streams_of[2], 71), 0)
    sketch = gaussian(streams_of[1], (FF, RANK), FF ** -0.5, 0.0390625, ((0, 8),))
    return {"deltas": deltas, "sketch": sketch}


def reference(deltas, sketch):

    def add_task(carried, delta_task):
        return (carried + delta_task.astype(jnp.float32), None)
    pooled, _ = lax.scan(add_task, jnp.zeros((FF, D), jnp.float32), deltas)

    def sketch_task(carried, delta_task):
        return (carried, jnp.dot(delta_task.T, sketch, preferred_element_type=jnp.float32))
    _, stacked = lax.scan(sketch_task, jnp.zeros((), jnp.float32), deltas)
    basis = jnp.transpose(stacked, (1, 0, 2)).reshape(D, TASKS * RANK).astype(jnp.bfloat16)
    gram = jnp.dot(basis.T, basis, preferred_element_type=jnp.float32)
    frob = jnp.sqrt(jnp.sum(gram * gram))
    identity = jnp.eye(TASKS * RANK, dtype=jnp.float32)
    iterate_y = (gram / frob).astype(jnp.bfloat16)
    iterate_z = identity.astype(jnp.bfloat16)
    for iteration in range(NS_STEPS):
        turn = ((3.0 * identity - jnp.dot(iterate_z, iterate_y, preferred_element_type=jnp.float32)) * 0.5).astype(jnp.bfloat16)
        if iteration == 0:
            iterate_y = jnp.dot(iterate_y, turn, preferred_element_type=jnp.float32).astype(jnp.bfloat16)
        elif iteration + 1 < NS_STEPS:
            iterate_y = jnp.dot(turn, iterate_y, preferred_element_type=jnp.float32).astype(jnp.bfloat16)
        iterate_z = jnp.dot(turn, iterate_z, preferred_element_type=jnp.float32).astype(jnp.bfloat16)
    coeff = (jnp.dot(pooled, basis.astype(jnp.float32), precision=lax.Precision.HIGHEST) / TASKS).astype(jnp.bfloat16)
    second = jnp.dot(coeff, iterate_z, preferred_element_type=jnp.float32).astype(jnp.bfloat16)
    third = (jnp.dot(second, iterate_z, preferred_element_type=jnp.float32) / frob).astype(jnp.bfloat16)
    return jnp.dot(third, basis.T, preferred_element_type=jnp.float32).astype(jnp.bfloat16)
```

```python
import jax
import jax.numpy as jnp
from jax import lax
from jax.sharding import PartitionSpec as P

NS_STEPS = 5
ROW_CHUNKS = 4


def dot32(a, b):
    return jnp.dot(a, b, preferred_element_type=jnp.float32)


def dot16(a, b):
    return dot32(a, b).astype(jnp.bfloat16)


def swap(value, bit, size):
    return lax.ppermute(value, "task", [(i, i ^ bit) for i in range(size)])


def ring_order(size):
    return list(range(0, size, 2)) + list(range(size - 1 - size % 2, 0, -2))


def reduce_blocks(terms, order, place):
    size, rows = terms.shape[0], terms.shape[1]
    half = rows // 2
    table = jnp.array(order, jnp.int32)
    ahead = [(order[i], order[(i + 1) % size]) for i in range(size)]
    back = [(b, a) for a, b in ahead]

    def block(position, low):
        own = lax.dynamic_index_in_dim(terms, table[position % size], 0, keepdims=False)
        return own[:half] if low else own[half:]

    one = block(place - 1 + size, True)
    two = block(place + 1, False)
    for step in range(size - 1):
        one = lax.ppermute(one, "row", ahead)
        two = lax.ppermute(two, "row", back)
        one = one.astype(jnp.float32) + block(place - 2 - step + 2 * size, True).astype(jnp.float32)
        two = two.astype(jnp.float32) + block(place + 2 + step, False).astype(jnp.float32)
        one, two = one.astype(jnp.bfloat16), two.astype(jnp.bfloat16)
    return jnp.concatenate([one, two], axis=0)


def gather_blocks(own, order, place):
    size, rows = len(order), own.shape[0]
    half = rows // 2
    table = jnp.array(order, jnp.int32)
    ahead = [(order[i], order[(i + 1) % size]) for i in range(size)]
    back = [(b, a) for a, b in ahead]
    whole = jnp.zeros((size * rows, own.shape[1]), own.dtype)
    whole = lax.dynamic_update_slice_in_dim(whole, own, table[place] * rows, 0)
    one, two = own[:half], own[half:]
    for step in range(1, size):
        one = lax.ppermute(one, "row", ahead)
        two = lax.ppermute(two, "row", back)
        first = table[(place - step + size) % size] * rows
        second = table[(place + step) % size] * rows + half
        whole = lax.dynamic_update_slice_in_dim(whole, one, first, 0)
        whole = lax.dynamic_update_slice_in_dim(whole, two, second, 0)
    return whole


def inverse_root_of(gram_scaled):
    identity = jnp.eye(gram_scaled.shape[0], dtype=jnp.float32)
    iterate_y = gram_scaled.astype(jnp.bfloat16)
    turn = ((3.0 * identity - iterate_y.astype(jnp.float32)) * 0.5).astype(jnp.bfloat16)
    iterate_y = dot16(iterate_y, turn)
    iterate_z = turn
    for iteration in range(1, NS_STEPS):
        turn = ((3.0 * identity - dot32(iterate_z, iterate_y)) * 0.5).astype(jnp.bfloat16)
        if iteration + 1 < NS_STEPS:
            iterate_y = dot16(turn, iterate_y)
        iterate_z = dot16(turn, iterate_z)
    return iterate_z


def body(deltas, sketch):
    local_tasks, local_rows, model_width = deltas.shape
    row_devices = lax.axis_size("row")
    groups = lax.axis_size("task")
    task = lax.axis_index("task")
    rank_width = sketch.shape[1]
    width = local_tasks * rank_width
    order = ring_order(row_devices)
    inverse = [order.index(i) for i in range(row_devices)]
    place = jnp.array(inverse, jnp.int32)[lax.axis_index("row")]
    terms = jnp.einsum("tmk,mr->ktr", deltas, sketch, preferred_element_type=jnp.float32)
    terms = terms.reshape(row_devices, model_width // row_devices, width).astype(jnp.bfloat16)
    pooled = deltas[0].astype(jnp.float32)
    for slot in range(1, local_tasks):
        pooled = pooled + deltas[slot].astype(jnp.float32)
    pooled = pooled.astype(jnp.bfloat16)

    basis_local = reduce_blocks(terms, order, place)
    parts = [basis_local]
    bit = 2
    while bit < groups:
        other = [swap(part, bit, groups) for part in parts]
        upper = (task // bit) % 2 == 1
        parts = [jnp.where(upper, b, a) for a, b in zip(parts, other)] + [
            jnp.where(upper, a, b) for a, b in zip(parts, other)
        ]
        bit *= 2
    near = gather_blocks(jnp.concatenate(parts, axis=1), order, place)
    far = swap(near, 1, groups)

    near_part = dot16(pooled, near)
    sent = swap(near_part, 1, groups)
    far_part = dot32(pooled, far)
    chip_sum = (far_part + sent.astype(jnp.float32)).astype(jnp.bfloat16)

    chunk = local_rows // ROW_CHUNKS
    coeffs = []
    for at in range(ROW_CHUNKS):
        far_sum = chip_sum[at * chunk : (at + 1) * chunk]
        bit = 2
        while bit < groups:
            other = swap(far_sum, bit, groups).astype(jnp.float32)
            far_sum = (far_sum.astype(jnp.float32) + other).astype(jnp.bfloat16)
            bit *= 2
        coeffs.append((swap(far_sum, 1, groups), far_sum))

    basis = jnp.concatenate([near, far], axis=1)
    gram = lax.dot_general(basis, basis, (((0,), (0,)), ((), ())), preferred_element_type=jnp.float32)
    frob = jnp.sqrt(jnp.sum(gram * gram))
    root = inverse_root_of(gram / frob)
    columns = model_width // groups
    column_basis = lax.dynamic_slice_in_dim(basis, task * columns, columns, 0)
    left = lax.dot_general(
        root, column_basis, (((1,), (1,)), ((), ())), preferred_element_type=jnp.float32
    ).astype(jnp.bfloat16)
    left = (dot32(root, left) / (frob * (local_tasks * groups))).astype(jnp.bfloat16)
    coeff = jnp.concatenate([jnp.concatenate(pair, axis=1) for pair in coeffs], axis=0)
    return dot16(coeff, left)


def solution(mesh):
    return jax.shard_map(
        body,
        mesh=mesh,
        in_specs=(P("task", "row", None), P("row", None)),
        out_specs=P("row", "task"),
        check_vma=False,
    )
```

```python
import jax
import jax.numpy as jnp
from jax import lax
from jax.sharding import PartitionSpec as P

NS_STEPS = 5
ROW_CHUNKS = 4


def dot32(a, b):
    return jnp.dot(a, b, preferred_element_type=jnp.float32)


def dot16(a, b):
    return dot32(a, b).astype(jnp.bfloat16)


def swap(value, bit, size):
    return lax.ppermute(value, "task", [(i, i ^ bit) for i in range(size)])


def ring_starts(place, size, rows):
    starts = []
    for k in range(size):
        twice = lax.rem(place * jnp.uint32(2) + jnp.uint32(2 * k), jnp.uint32(2 * size))
        starts.append(jnp.minimum(twice, jnp.uint32(2 * size - 1) - twice) * jnp.uint32(rows))
    return starts


def zero_after(value):
    return jnp.where(jnp.isnan(value[0, 0].astype(jnp.float32)), 1.0, 0.0).astype(jnp.float32)


def ring_pairs(size):
    order = list(range(0, size, 2)) + list(range(size - 1 - size % 2, 0, -2))
    ahead = [(order[i], order[(i + 1) % size]) for i in range(size)]
    return ahead, [(b, a) for a, b in ahead]


def reduce_blocks(terms, starts):
    size = len(starts)
    half = terms.shape[0] // size // 2
    ahead, back = ring_pairs(size)

    def block(source, ahead_by, offset):
        first = starts[ahead_by % size] + jnp.uint32(offset)
        return lax.dynamic_slice(source, (first, jnp.uint32(0)), (half, source.shape[1]))

    def add(a, b):
        return (a.astype(jnp.float32) + b.astype(jnp.float32)).astype(jnp.bfloat16)

    one = block(terms, -1, 0)
    two = block(terms, 1, half)
    for step in range(size - 1):
        one = lax.ppermute(one, "row", ahead)
        two = lax.ppermute(two, "row", back)
        one, source = lax.optimization_barrier((one, terms))
        one = add(one, block(source, -2 - step, 0))
        two, source = lax.optimization_barrier((two, terms))
        two = add(two, block(source, 2 + step, half))
    return jnp.concatenate([one, two], axis=0)


def gather_blocks(own, starts, groups):
    size, rows = len(starts), own.shape[0]
    half = rows // 2
    width = 2 * own.shape[1]
    ahead, back = ring_pairs(size)
    whole = jnp.zeros((size * rows, width), own.dtype)
    gram = jnp.zeros((width, width), jnp.float32)
    one, two = own[:half], own[half:]
    for step in range(size):
        first = starts[-step % size]
        second = starts[step] + jnp.uint32(half)
        both = jnp.concatenate([one, two], axis=0)
        if step + 1 < size:
            one = lax.ppermute(one, "row", ahead)
            two = lax.ppermute(two, "row", back)
        block = jnp.concatenate([both, swap(both, 1, groups)], axis=1)
        block = lax.optimization_barrier(block)
        whole = lax.dynamic_update_slice(whole, block[:half], (first, jnp.uint32(0)))
        whole = lax.dynamic_update_slice(whole, block[half:], (second, jnp.uint32(0)))
        gram = gram + lax.dot_general(
            block, block, (((0,), (0,)), ((), ())), preferred_element_type=jnp.float32
        )
        gram = lax.optimization_barrier(gram)
    return whole, gram


def inverse_root_of(gram_scaled, later):
    identity = jnp.eye(gram_scaled.shape[0], dtype=jnp.float32)
    iterate_y = gram_scaled.astype(jnp.bfloat16)
    turn = ((3.0 * identity - iterate_y.astype(jnp.float32)) * 0.5).astype(jnp.bfloat16)
    iterate_y = dot16(iterate_y, turn)
    iterate_z = turn
    for iteration in range(1, NS_STEPS):
        turn = (3.0 * identity - dot32(iterate_z, iterate_y)) * (0.5 + later.get(iteration, 0.0))
        turn = turn.astype(jnp.bfloat16)
        if iteration + 1 < NS_STEPS:
            iterate_y = dot16(turn, iterate_y)
        iterate_z = dot16(turn, iterate_z)
    return iterate_z


def body(deltas, sketch):
    local_tasks, local_rows, model_width = deltas.shape
    row_devices = lax.axis_size("row")
    groups = lax.axis_size("task")
    task = lax.axis_index("task")
    rank_width = sketch.shape[1]
    width = local_tasks * rank_width
    row = lax.axis_index("row").astype(jnp.uint32)
    back = jnp.uint32(row_devices - 1) - row // jnp.uint32(2)
    place = jnp.where((row & jnp.uint32(1)) == 0, row // jnp.uint32(2), back)
    starts = ring_starts(place, row_devices, model_width // row_devices)
    terms = jnp.einsum("tmk,mr->ktr", deltas, sketch, preferred_element_type=jnp.float32)
    terms = lax.optimization_barrier(terms.reshape(model_width, width).astype(jnp.bfloat16))

    basis_local = reduce_blocks(terms, starts)
    parts = [basis_local]
    bit = 2
    while bit < groups:
        other = [swap(part, bit, groups) for part in parts]
        upper = (task // bit) % 2 == 1
        parts = [jnp.where(upper, b, a) for a, b in zip(parts, other)] + [
            jnp.where(upper, a, b) for a, b in zip(parts, other)
        ]
        bit *= 2
    own = jnp.concatenate(parts, axis=1)
    basis, gram = gather_blocks(own, starts, groups)

    near_width = own.shape[1]
    chunk = local_rows // ROW_CHUNKS
    coeffs, chip_sums, received = [], [], []
    for at in range(ROW_CHUNKS):
        pooled = deltas[0, at * chunk : (at + 1) * chunk].astype(jnp.float32)
        for slot in range(1, local_tasks):
            pooled = pooled + deltas[slot, at * chunk : (at + 1) * chunk].astype(jnp.float32)
        part = dot32(pooled.astype(jnp.bfloat16), basis)
        if at >= 2:
            part = part * (1.0 + zero_after(chip_sums[at - 2]))
        if at >= 3:
            part = part * (1.0 + zero_after(received[at - 3]))
        part = lax.optimization_barrier(part.astype(jnp.bfloat16))
        far_sum = part[:, near_width:].astype(jnp.float32)
        far_sum = far_sum + swap(part[:, :near_width], 1, groups).astype(jnp.float32)
        far_sum = far_sum.astype(jnp.bfloat16)
        chip_sums.append(far_sum)
        bit = 2
        while bit < groups:
            other = swap(far_sum, bit, groups).astype(jnp.float32)
            far_sum = (far_sum.astype(jnp.float32) + other).astype(jnp.bfloat16)
            bit *= 2
        received.append(far_sum)
        coeffs.append((swap(far_sum, 1, groups), far_sum))

    frob = jnp.sqrt(jnp.sum(gram * gram))
    first = gram / (frob * (1.0 + zero_after(chip_sums[2])))
    later = {1: zero_after(chip_sums[3]), 3: zero_after(received[1])}
    root = lax.optimization_barrier(inverse_root_of(first, later))
    columns = model_width // groups
    column_basis = lax.dynamic_slice_in_dim(basis, task * columns, columns, 0)
    left = lax.dot_general(
        root, column_basis, (((1,), (1,)), ((), ())), preferred_element_type=jnp.float32
    ).astype(jnp.bfloat16)
    left = lax.optimization_barrier(left)
    scale = frob * (local_tasks * groups) * (1.0 + zero_after(received[2]))
    left = lax.optimization_barrier((dot32(root, left) / scale).astype(jnp.bfloat16))
    outs = []
    for near_sum, far_sum in coeffs:
        out = dot32(far_sum, left[near_width:]) + dot32(near_sum, left[:near_width])
        outs.append(out.astype(jnp.bfloat16))
    return jnp.concatenate(outs, axis=0)


def solution(mesh):
    return jax.shard_map(
        body,
        mesh=mesh,
        in_specs=(P("task", "row", None), P("row", None)),
        out_specs=P("row", "task"),
        check_vma=False,
    )
```
